32 devices in a mesh: dp: 4 (over y, core), expert: 2 (over x), tensor: 4 (over z).
Axes of the slice: x: 2, y: 2, z: 4, core: 2. Of those that a mesh axis runs over, the one named last changes fastest.
Arguments:
- tokens: bfloat16 [16, 1024, 768], P(('dp', 'expert')), may hold values from -6 to 6
- segments: int32 [16, 1024], P(('dp', 'expert')), may hold values from 0 to 3, never falling along the last dimension, each value on 1 to 512 neighbouring positions
- routes: int32 [16, 1024, 1], P(('dp', 'expert')), may hold values from 0 to 1; in each aligned block of 2048 rows (0 to 2047, 2048 to 4095, ..., all dimensions but the last counted through in order) at most 1280 rows name the same one
- rel_bucket: int32 [2047], replicated, may hold values from 0 to 31, as said below
- norm1_gain: bfloat16 [768], replicated, may hold values from 0.5 to 1.5
- query_key_value_weight: bfloat16 [768, 3, 768], P(None, None, 'tensor'), may hold values from -0.21875 to 0.21875
- output_weight: bfloat16 [768, 768], P(None, 'tensor'), may hold values from -3.5 to 3.5
- bias_table: bfloat16 [32, 12], P(None, 'tensor'), may hold values from -4 to 4
- norm2_gain: bfloat16 [768], replicated, may hold values from 0.5 to 1.5
- w_router: bfloat16 [768, 2], replicated, may hold values from -0.109375 to 0.109375
- w_in: bfloat16 [2, 768, 3072], P('expert', None, 'tensor'), may hold values from -0.21875 to 0.21875
- w_expert_out: bfloat16 [2, 768, 3072], P('expert', None, 'tensor'), may hold values from -0.21875 to 0.21875
- cotangent: bfloat16 [16, 1024, 768], P(('dp', 'expert')), may hold values from -6 to 6
Outputs:
- output: bfloat16 [16, 1024, 768], P(('dp', 'expert'))
- input_grad: bfloat16 [16, 1024, 768], P(('dp', 'expert'))
- grad_norm1: float32 [768], P(('dp', 'expert'))
- grad_qkv: float32 [768, 3, 768], P(('dp', 'expert'), None, 'tensor')
- grad_out: float32 [768, 768], P(('dp', 'expert'), 'tensor')
- grad_table: float32 [32, 12], P(None, 'tensor')
- grad_norm2: float32 [768], P(('dp', 'expert'))
- grad_router: float32 [768, 2], P(('dp', 'expert'))
- grad_in: float32 [2, 768, 3072], P('expert', 'dp', 'tensor')
- grad_expert_out: float32 [2, 768, 3072], P('expert', 'dp', 'tensor')
The draws below stay inside these ranges and needn't reach their ends.
Inputs may be any that keep to these rules, and one draw needn't show every extreme that they name: `routes`: in the 2048 tokens of one device (aligned blocks) no expert is named by more than 1280 tokens, a bound that some block reaches. `segments`: never falls along a sequence; each document has 1 to 512 tokens. `rel_bucket`: offsets r <= 0 take buckets 0 to 15 and offsets r > 0 buckets 16 to 31; within each sign the bucket never falls as |r| grows and equals |r| (plus 16 for r > 0) for |r| < 8.
All inputs are finite; a program needn't handle non-finite values.
Results may differ from the reference program's by a relative error of at most 0.017.
Values may be sent and summed in bfloat16 or wider, within the bound.
A program may use at most 192 MiB of HBM per device.

```python
import math
import jax
import jax.numpy as jnp
import numpy as np
from jax import lax

D = 768
HEADS = 12
HD = 64
FF = 3072
BUCKETS = 32
EXPERTS = 2
LEN = 1024
SEQ_DEV = 2
TOK_DEV = 2048
SEQS = 16
CAP = 1280


def draw_rel_bucket(key, part):
    key = jax.random.fold_in(key, 7)
    cuts = jax.random.permutation(key, LEN - 9)[:7].astype(jnp.int32) + 9
    offsets = jnp.arange(2 * LEN - 1, dtype=jnp.int32) - (LEN - 1)
    distance = jnp.abs(offsets)
    beyond = jnp.sum((distance[:, None] >= cuts[None, :]).astype(jnp.int32), axis=1)
    half_bucket = jnp.where(distance < 8, distance, 8 + beyond)
    return (half_bucket + 16 * (offsets > 0).astype(jnp.int32)).astype(jnp.int32)


def steps_of(rng, shape, pieces, smallest, largest):
    loudness = 1.0
    for axis_at, shards_of in pieces:
        heights = jax.random.uniform(jax.random.fold_in(jax.random.fold_in(rng, 6), axis_at), (shards_of,), jnp.float32, smallest / len(pieces), largest / len(pieces))
        loudness = loudness * jnp.repeat(jnp.exp(heights), shape[axis_at] // shards_of).reshape((-1,) + (1,) * (len(shape) - 1 - axis_at))
    return loudness


def length_profile(number_of, total, most, slope):
    weights = [(1 << 20) // math.isqrt(standing ** slope) + 1 for standing in range(2, number_of + 1)]
    rest, counts = total - most - (number_of - 1), [1] * (number_of - 1)
    while rest > 0:
        movable = [i for i in range(number_of - 1) if counts[i] < most]
        whole, left = sum([weights[i] for i in movable]), rest
        for i in movable:
            more = min(most - counts[i], max(1, left * weights[i] // whole), rest)
            counts[i] = counts[i] + more
            rest = rest - more
    return np.array([most] + counts)


def ragged(stream_key, count, total, most, skew):
    if count == 2:
        one = jax.random.randint(stream_key, (), max(1, total - most), min(most, total - 1) + 1)
        return jnp.stack([one, total - one])
    lengths = jnp.asarray(length_profile(count, total, most, skew), jnp.int32)
    twos = (count - 1) // 2
    donor, taker = lengths[1:1 + 2 * twos:2], lengths[2:2 + 2 * twos:2]
    margin = jnp.minimum(donor - 1, most - taker)
    moved = jax.random.randint(jax.random.fold_in(stream_key, 1), (twos,), 0, 1 << 20) % (margin + 1)
    lengths = lengths.at[1:1 + 2 * twos:2].set(donor - moved).at[2:2 + 2 * twos:2].set(taker + moved)
    return lengths[jax.random.permutation(jax.random.fold_in(stream_key, 2), count)]


def deal_out(own_key, own, number, rows, amount, top, bound, lean):
    order = jax.random.permutation(own_key, amount)
    crowded, ordinary = shares(amount, rows * top, bound, lean, True), shares(amount, rows * top, bound, lean, False)
    places = jnp.arange(amount)

    def named(lengths, rotation):
        used = int((lengths > 0).sum())
        fixed = max(1, used // 4)
        passed = fixed + (places - fixed + rotation * (used - fixed)) % max(1, amount - fixed)
        return jnp.zeros((amount,), jnp.int32).at[order[jnp.where(places < fixed, places, passed)]].set(jnp.asarray(lengths, jnp.int32))

    lengths = jnp.where(number % 4 == 0, named(crowded, number // 4), named(ordinary, number - number // 4 - 1))
    mixed = jax.random.permutation(jax.random.fold_in(own, 3), amount)
    donor, receiver = mixed[0:amount // 2 * 2:2], mixed[1:amount // 2 * 2:2]
    room = jnp.minimum(lengths[donor] - 1, bound - lengths[receiver]) // 2
    room = jnp.where((donor == order[0]) | (receiver == order[0]) | (lengths[receiver] == 0), 0, jnp.maximum(room, 0))
    passed = jax.random.randint(jax.random.fold_in(own, 4), (amount // 2,), 0, 1 << 20) % (room + 1)
    lengths = lengths.at[donor].add(-passed).at[receiver].add(passed)
    labels = jnp.searchsorted(jnp.cumsum(lengths), jnp.arange(rows * top), side="right").astype(jnp.int32)
    grid = labels.reshape(top, rows).T
    grid = grid[jax.random.permutation(jax.random.fold_in(own, 1), rows)]
    rotation = jax.random.randint(jax.random.fold_in(own, 2), (rows, 1), 0, top)
    return jnp.take_along_axis(grid, (jnp.arange(top)[None, :] + rotation) % top, axis=1)


def shares(count, total, most, skew, full):
    loads = [(1 << 20) // math.isqrt(grade ** skew) + 1 for grade in range(1, count + 1)]
    largest = most if full else min(most, max(-(-total // count), total * loads[0] // sum(loads)))
    least = 1 if total - largest >= count - 1 else 0
    given, rest = [largest] + [least] * (count - 1), total - largest - least * (count - 1)
    while rest > 0:
        candidates = [i for i in range(1, count) if given[i] < largest] or [i for i in range(1, count) if given[i] < most]
        whole, left = sum([loads[i] for i in candidates]), rest
        for i in candidates:
            more = min(most - given[i], max(1, left * loads[i] // whole), rest)
            given[i] = given[i] + more
            rest = rest - more
    return np.array(given)


def centred(own_key, shape, scale, limit, cuts=(), kind=jnp.bfloat16):
    entries = scale * jax.random.normal(own_key, shape, jnp.float32)
    if cuts:
        entries = entries * steps_of(own_key, shape, cuts, -0.22, 0.18)
    return jnp.clip(entries, -limit, limit).astype(kind)


def setup_inputs(seed: int = 0) -> dict:
    key_list = jax.random.split(jax.random.key(seed), 14)
    tokens = centred(key_list[0], (SEQS, LEN, D), 1.0, 6.0, ((0, 8),))
    segments = jax.vmap(lambda own: jnp.searchsorted(jnp.cumsum(ragged(own, 4, LEN, LEN // 2, 0)), jnp.arange(LEN), side="right"))(jax.random.split(key_list[1], SEQS)).reshape((SEQS, LEN)).astype(jnp.int32)
    routes_keys = jax.random.split(jax.random.fold_in(key_list[2], 1), SEQS * LEN // TOK_DEV)
    routes_turns = jax.random.permutation(jax.random.fold_in(key_list[2], 3), SEQS * LEN // TOK_DEV)
    routes = jax.vmap(lambda own, number: deal_out(jax.random.fold_in(key_list[2], 2), own, number, TOK_DEV, EXPERTS, 1, CAP, 2))(routes_keys, routes_turns).reshape((SEQS, LEN, 1))
    rel_bucket = draw_rel_bucket(jax.random.fold_in(key_list[13], 71), 0)
    norm1_gain = jnp.clip(1.0 + 0.1 * jax.random.normal(key_list[4], (D,), jnp.float32), 0.5, 1.5).astype(jnp.bfloat16)
    query_key_value_weight = centred(key_list[5], (D, 3, HEADS * HD), D ** -0.5, 0.21875, ((2, 4),))
    output_weight = centred(key_list[6], (D, HEADS * HD), (max(4 * HEADS * HD // LEN, 1)) ** -0.5, 3.5, ((1, 4),))
    bias_table = centred(key_list[7], (BUCKETS, HEADS), 1.0, 4.0, ((1, 4),))
    norm2_gain = jnp.clip(1.0 + 0.1 * jax.random.normal(key_list[8], (D,), jnp.float32), 0.5, 1.5).astype(jnp.bfloat16)
    w_router = centred(key_list[9], (D, EXPERTS), (4 * D) ** -0.5, 0.109375)
    w_in = centred(key_list[10], (EXPERTS, D, FF), D ** -0.5, 0.21875, ((0, 2), (2, 4)))
    w_expert_out = centred(key_list[11], (EXPERTS, D, FF), (max(FF // (EXPERTS * EXPERTS), 1)) ** -0.5, 0.21875, ((0, 2), (2, 4)))
    cotangent = centred(key_list[12], (SEQS, LEN, D), 1.0, 6.0, ((0, 8),))
    return dict(tokens=tokens, segments=segments, routes=routes, rel_bucket=rel_bucket, norm1_gain=norm1_gain, query_key_value_weight=query_key_value_weight, output_weight=output_weight, bias_table=bias_table, norm2_gain=norm2_gain, w_router=w_router, w_in=w_in, w_expert_out=w_expert_out, cotangent=cotangent)


HIGHEST_PRECISE = lax.Precision.HIGHEST

@jax.custom_vjp
def low(v):
    return lax.optimization_barrier(v.astype(jnp.bfloat16)).astype(jnp.float32)

@jax.custom_vjp
def low_back(v):
    return v

def low_keep(v):
    return (low(v), None)

def low_pass(kept, grad):
    return (grad,)

def back_keep(v):
    return (v, None)

def back_low(kept, grad):
    return (low(grad),)
low.defvjp(low_keep, low_pass)
low_back.defvjp(back_keep, back_low)

def smooth(values_in):
    return 0.5 * values_in * (1.0 + jnp.tanh(0.7978845608028654 * (values_in + 0.044715 * values_in * values_in * values_in)))

def normed(values_in, gain_vec):
    return values_in * lax.rsqrt(lax.optimization_barrier(jnp.mean(values_in * values_in, axis=-1, keepdims=True)) + 1e-06) * gain_vec

def attend(queries, keys, values, rel_bias, segments):
    seq_count, length = (queries.shape[0], queries.shape[1])
    block_rows = min(512, length)
    key_pos = jnp.arange(length, dtype=jnp.int32)
    score_scale = 1.0 / jnp.sqrt(jnp.float32(HD))

    def one_block(start):
        query_blk = lax.dynamic_slice_in_dim(queries, start, block_rows, 1)
        seg_blk = lax.dynamic_slice_in_dim(segments, start, block_rows, 1)
        query_pos = start + jnp.arange(block_rows, dtype=jnp.int32)
        rel_index = key_pos[None, :] - query_pos[:, None] + (length - 1)
        bias_blk = jnp.take(rel_bias, rel_index, axis=1)
        raw_scores = jnp.einsum('sqhd,skhd->shqk', query_blk, keys, precision=HIGHEST_PRECISE) * score_scale + bias_blk[None]
        raw_scores = low_back(raw_scores)
        same_doc = (seg_blk[:, :, None] == segments[:, None, :])[:, None]
        masked = jnp.where(same_doc, raw_scores, -1e+30)
        prob_blk = jax.nn.softmax(masked, axis=-1)
        return jnp.einsum('shqk,skhd->sqhd', low(prob_blk), values, precision=HIGHEST_PRECISE)
    starts = jnp.arange(length // block_rows, dtype=jnp.int32) * block_rows
    stacked = lax.map(jax.checkpoint(one_block), starts)
    return jnp.moveaxis(stacked, 0, 1).reshape(seq_count, length, -1)

def layer(inputs, norm1_gain, query_key_value_weight, output_weight, bias_table, norm2_gain, w_router, w_in, w_expert_out, segments, chosen, flat_place, bucket_hot):
    seq_count, length, model_width = inputs.shape
    tok_count = seq_count * length
    attention_input = low(normed(inputs, norm1_gain))
    query_key_value = low_back(low(jnp.einsum('uhg,gby->uhby', attention_input, query_key_value_weight, precision=HIGHEST_PRECISE)))
    queries = query_key_value[:, :, 0].reshape(seq_count, length, HEADS, HD)
    keys = query_key_value[:, :, 1].reshape(seq_count, length, HEADS, HD)
    values = query_key_value[:, :, 2].reshape(seq_count, length, HEADS, HD)
    rel_bias = jnp.dot(bucket_hot, bias_table, precision=HIGHEST_PRECISE).T
    mixed_values = low_back(low(attend(queries, keys, values, rel_bias, segments)))
    attention_output = low_back(jnp.einsum('ahw,ow->aho', mixed_values, output_weight, precision=HIGHEST_PRECISE))
    residual = inputs + attention_output
    moe_in = low(normed(residual, norm2_gain)).reshape(tok_count, model_width)
    logits = jnp.dot(moe_in, w_router, precision=HIGHEST_PRECISE)
    gate_value = lax.optimization_barrier(jnp.sum(jax.nn.softmax(logits, axis=-1) * chosen, axis=-1))
    routed = low_back(moe_in)
    slot_buffer = jnp.zeros((EXPERTS * CAP, model_width), jnp.float32).at[flat_place].set(routed)
    slot_buffer = slot_buffer.reshape(EXPERTS, CAP, model_width)
    hidden = low_back(jnp.einsum('ecd,edf->ecf', slot_buffer, w_in, precision=HIGHEST_PRECISE))
    active = low(smooth(hidden))
    expert_out = low_back(low(jnp.einsum('ecf,edf->ecd', active, w_expert_out, precision=HIGHEST_PRECISE)))
    picked = expert_out.reshape(EXPERTS * CAP, model_width)[flat_place]
    return residual + (gate_value[:, None] * picked).reshape(seq_count, length, model_width)

def reference(tokens, segments, routes, rel_bucket, norm1_gain, query_key_value_weight, output_weight, bias_table, norm2_gain, w_router, w_in, w_expert_out, cotangent):
    block_count = SEQS // SEQ_DEV
    params = tuple((param.astype(jnp.float32) for param in (norm1_gain, query_key_value_weight, output_weight, bias_table, norm2_gain, w_router, w_in, w_expert_out)))
    bucket_hot = (rel_bucket[:, None] == jnp.arange(BUCKETS, dtype=jnp.int32)[None, :]).astype(jnp.float32)
    token_blocks = tokens.astype(jnp.float32).reshape(block_count, SEQ_DEV, LEN, D)
    cot_blocks = cotangent.astype(jnp.float32).reshape(block_count, SEQ_DEV, LEN, D)
    seg_blocks = segments.reshape(block_count, SEQ_DEV, LEN)
    route_blocks = routes.reshape(block_count, TOK_DEV)

    def one_device(grads, item):
        inputs, grad_output, seg_blk, route_blk = item
        chosen_int = (route_blk[:, None] == jnp.arange(EXPERTS, dtype=jnp.int32)[None, :]).astype(jnp.int32)
        slot_rank = lax.optimization_barrier(jnp.sum((jnp.cumsum(chosen_int, axis=0) - 1) * chosen_int, axis=1))
        flat_place = (route_blk * CAP + slot_rank).astype(jnp.int32)
        chosen = chosen_int.astype(jnp.float32)

        def forward(inputs_in, *weights):
            return layer(inputs_in, *weights, seg_blk, chosen, flat_place, bucket_hot)
        result, pullback = jax.vjp(forward, inputs, *params)
        cotangents = pullback(grad_output)
        new_grads = tuple((total + piece for total, piece in zip(grads, cotangents[1:])))
        return (new_grads, (result.astype(jnp.bfloat16), cotangents[0].astype(jnp.bfloat16)))
    zero_grads = tuple((jnp.zeros(param.shape, jnp.float32) for param in params))
    grads, (out_blocks, in_grad_blocks) = lax.scan(one_device, zero_grads, (token_blocks, cot_blocks, seg_blocks, route_blocks))
    output = out_blocks.reshape(SEQS, LEN, D)
    input_grad = in_grad_blocks.reshape(SEQS, LEN, D)
    return (output, input_grad, grads[0], grads[1], grads[2], grads[3], grads[4], grads[5], grads[6], grads[7])
```

```python
import functools
import math

import jax
import jax.numpy as jnp
from jax import lax
from jax.experimental import pallas as pl
from jax.experimental.pallas import tpu as pltpu
from jax.sharding import PartitionSpec as P

HIGHEST_PRECISE = lax.Precision.HIGHEST
PAIR = 2
SUB = 128


def smooth(values_in):
    return (
        0.5
        * values_in
        * (
            1.0
            + jnp.tanh(
                0.7978845608028654 * (values_in + 0.044715 * values_in * values_in * values_in)
            )
        )
    )


def normed(values_in, gain_vec):
    return (
        values_in
        * lax.rsqrt(jnp.mean(values_in * values_in, axis=-1, keepdims=True) + 1e-06)
        * gain_vec
    )


def dot_nt(a, b):
    return lax.dot_general(a, b, (((1,), (1,)), ((), ())), preferred_element_type=jnp.float32)


def dot_nn(a, b):
    return jnp.dot(a, b, preferred_element_type=jnp.float32)


def build_bias(row, bias_buf):
    wide = jnp.broadcast_to(row, bias_buf.shape)
    bias_buf[...] = pltpu.roll(wide, 0, 1, stride=1, stride_axis=0)


def forward_kernel(hs, rows, q_ref, k_ref, v_ref, bias_ref, segq_ref, segk_ref, o_ref, lse_ref, bias_buf):
    length = k_ref.shape[0]
    scale = 1.0 / math.sqrt(hs)
    for h in range(PAIR):
        build_bias(bias_ref[h], bias_buf)
        cols = slice(h * hs, (h + 1) * hs)
        k_h = k_ref[:, cols]
        v_h = v_ref[:, cols]
        for b in range(rows // SUB):
            at = slice(b * SUB, (b + 1) * SUB)
            off = rows - b * SUB
            s = dot_nt(q_ref[at, cols], k_h) * scale + bias_buf[:, off : off + length]
            s = jnp.where(segq_ref[at, :] == segk_ref[...], s, -1e30)
            top = jnp.max(s, axis=-1, keepdims=True)
            e = jnp.exp(s - top)
            total = jnp.sum(e, axis=-1, keepdims=True)
            p = (e * (1.0 / total)).astype(jnp.bfloat16)
            o_ref[at, cols] = dot_nn(p, v_h).astype(jnp.bfloat16)
            lse_ref[h, at, :] = top + jnp.log(total)


def backward_kernel(
    hs, rows, q_ref, k_ref, v_ref, g_ref, bias_ref, segq_ref, segk_ref, lse_ref,
    dq_ref, dk_ref, dv_ref, drel_ref, bias_buf, drel_buf, p_buf, ds_buf,
):
    length = k_ref.shape[0]
    scale = 1.0 / math.sqrt(hs)
    width = bias_buf.shape[1]
    q_t = q_ref[...].T
    g_t = g_ref[...].T
    for h in range(PAIR):
        build_bias(bias_ref[h], bias_buf)
        drel_buf[...] = jnp.zeros_like(drel_buf)
        cols = slice(h * hs, (h + 1) * hs)
        k_h = k_ref[:, cols]
        v_h = v_ref[:, cols]
        for b in range(rows // SUB):
            at = slice(b * SUB, (b + 1) * SUB)
            off = rows - b * SUB
            s = dot_nt(q_ref[at, cols], k_h) * scale + bias_buf[:, off : off + length]
            s = jnp.where(segq_ref[at, :] == segk_ref[...], s, -1e30)
            p = jnp.exp(s - lse_ref[h, at, :])
            dp = dot_nt(g_ref[at, cols], v_h)
            ds = p * (dp - jnp.sum(p * dp, axis=-1, keepdims=True))
            ds = ds.astype(jnp.bfloat16)
            p_buf[at, :] = p.astype(jnp.bfloat16)
            ds_buf[at, :] = ds
            dq_ref[at, cols] = (dot_nn(ds, k_h) * scale).astype(jnp.bfloat16)
            drel_buf[:, off : off + length] += ds.astype(jnp.float32)
        dk_ref[cols, :] = dot_nn(q_t[cols, :], ds_buf[...]) * scale
        dv_ref[cols, :] = dot_nn(g_t[cols, :], p_buf[...])
        size = SUB
        while size > 8:
            size //= 2
            upper = pltpu.roll(drel_buf[size : 2 * size, :], width - size, 1)
            drel_buf[:size, :] += upper
        drel_ref[h] = drel_buf[:8, :]


def attend_forward(q, k, v, bias_rows, seg_q, seg_k, hs):
    rows, feats = q.shape
    length = k.shape[0]
    heads = feats // hs
    width = bias_rows.shape[2]
    lanes = PAIR * hs
    return pl.pallas_call(
        functools.partial(forward_kernel, hs, rows),
        grid=(heads // PAIR,),
        in_specs=[
            pl.BlockSpec((rows, lanes), lambda i: (0, i)),
            pl.BlockSpec((length, lanes), lambda i: (0, i)),
            pl.BlockSpec((length, lanes), lambda i: (0, i)),
            pl.BlockSpec((PAIR, 1, width), lambda i: (i, 0, 0)),
            pl.BlockSpec((rows, 1), lambda i: (0, 0)),
            pl.BlockSpec((1, length), lambda i: (0, 0)),
        ],
        out_specs=[
            pl.BlockSpec((rows, lanes), lambda i: (0, i)),
            pl.BlockSpec((PAIR, rows, 1), lambda i: (i, 0, 0)),
        ],
        out_shape=[
            jax.ShapeDtypeStruct((rows, feats), jnp.bfloat16),
            jax.ShapeDtypeStruct((heads, rows, 1), jnp.float32),
        ],
        scratch_shapes=[pltpu.VMEM((SUB, width), jnp.float32)],
        compiler_params=pltpu.CompilerParams(vmem_limit_bytes=40 * 1024 * 1024),
        cost_estimate=pl.CostEstimate(
            flops=4 * rows * length * feats, bytes_accessed=8 * length * feats,
            transcendentals=rows * length * heads,
        ),
        name="attend_forward",
    )(q, k, v, bias_rows, seg_q, seg_k)


def attend_backward(q, k, v, g, bias_rows, seg_q, seg_k, lse, hs):
    rows, feats = q.shape
    length = k.shape[0]
    heads = feats // hs
    width = bias_rows.shape[2]
    lanes = PAIR * hs
    return pl.pallas_call(
        functools.partial(backward_kernel, hs, rows),
        grid=(heads // PAIR,),
        in_specs=[
            pl.BlockSpec((rows, lanes), lambda i: (0, i)),
            pl.BlockSpec((length, lanes), lambda i: (0, i)),
            pl.BlockSpec((length, lanes), lambda i: (0, i)),
            pl.BlockSpec((rows, lanes), lambda i: (0, i)),
            pl.BlockSpec((PAIR, 1, width), lambda i: (i, 0, 0)),
            pl.BlockSpec((rows, 1), lambda i: (0, 0)),
            pl.BlockSpec((1, length), lambda i: (0, 0)),
            pl.BlockSpec((PAIR, rows, 1), lambda i: (i, 0, 0)),
        ],
        out_specs=[
            pl.BlockSpec((rows, lanes), lambda i: (0, i)),
            pl.BlockSpec((lanes, length), lambda i: (i, 0)),
            pl.BlockSpec((lanes, length), lambda i: (i, 0)),
            pl.BlockSpec((PAIR, 8, width), lambda i: (i, 0, 0)),
        ],
        out_shape=[
            jax.ShapeDtypeStruct((rows, feats), jnp.bfloat16),
            jax.ShapeDtypeStruct((feats, length), jnp.float32),
            jax.ShapeDtypeStruct((feats, length), jnp.float32),
            jax.ShapeDtypeStruct((heads, 8, width), jnp.float32),
        ],
        scratch_shapes=[
            pltpu.VMEM((SUB, width), jnp.float32),
            pltpu.VMEM((SUB, width), jnp.float32),
            pltpu.VMEM((rows, length), jnp.bfloat16),
            pltpu.VMEM((rows, length), jnp.bfloat16),
        ],
        compiler_params=pltpu.CompilerParams(vmem_limit_bytes=48 * 1024 * 1024),
        cost_estimate=pl.CostEstimate(
            flops=10 * rows * length * feats, bytes_accessed=20 * length * feats,
            transcendentals=rows * length * heads,
        ),
        name="attend_backward",
    )(q, k, v, g, bias_rows, seg_q, seg_k, lse)


def gather_rows(shard):
    copies = lax.axis_size("dp")
    part = shard.shape[0] // copies
    mine = lax.dynamic_slice_in_dim(shard, lax.axis_index("dp") * part, part, 0)
    return lax.all_gather(mine, ("tensor", "dp"), axis=0, tiled=True)


def per_device(
    tokens,
    segments,
    routes,
    rel_bucket,
    norm1_gain,
    query_key_value_weight,
    output_weight,
    bias_table,
    norm2_gain,
    w_router,
    w_in,
    w_expert_out,
    cotangent,
):
    seq_count, length, model_width = tokens.shape
    tok_count = seq_count * length
    heads_here = bias_table.shape[1]
    bucket_count = bias_table.shape[0]
    head_feat = query_key_value_weight.shape[2]
    hs = head_feat // heads_here
    experts = w_router.shape[1]
    local_exp = w_in.shape[0]
    ff_here = w_in.shape[2]
    peers = lax.axis_size("expert")
    splits = lax.axis_size("tensor")
    feats = head_feat * splits
    heads = heads_here * splits
    rank = lax.axis_index("tensor")
    capacity = tok_count * 5 // (4 * experts)
    share = tok_count // splits
    slots = min(capacity, share)
    per_seq = length // share
    seq_at = rank // per_seq
    seq_rank = rank % per_seq
    q_start = seq_rank * share
    own_start = rank * share

    def own(rows):
        return lax.dynamic_slice_in_dim(rows, own_start, share, 0)

    w_qkv_t = jnp.transpose(query_key_value_weight, (1, 2, 0)).reshape(3 * head_feat, model_width)
    table_rows = jnp.pad(bias_table.T, ((0, 64 - heads_here), (0, model_width - bucket_count)))
    qkv_all = gather_rows(jnp.concatenate([w_qkv_t, table_rows], 0))
    qkv_all = qkv_all.reshape(splits, 3 * head_feat + 64, model_width)
    table_all = qkv_all[:, 3 * head_feat : 3 * head_feat + heads_here, :bucket_count]
    table_all = table_all.reshape(heads, bucket_count).astype(jnp.float32)
    qkv_all = [
        qkv_all[:, c * head_feat : (c + 1) * head_feat].reshape(feats, model_width)
        for c in range(3)
    ]
    w_out_all = lax.all_gather(output_weight.T, "tensor", axis=0, tiled=True)
    w_in_all = gather_rows(w_in.reshape(local_exp * model_width, ff_here).T)
    w_eout_all = gather_rows(w_expert_out.reshape(local_exp * model_width, ff_here).T)

    gain_one = norm1_gain.astype(jnp.float32)
    gain_two = norm2_gain.astype(jnp.float32)
    seq_tokens = lax.dynamic_index_in_dim(tokens, seq_at, 0, keepdims=False).astype(jnp.float32)
    seq_seg = lax.dynamic_index_in_dim(segments, seq_at, 0, keepdims=False)
    a_in = normed(seq_tokens, gain_one).astype(jnp.bfloat16)
    x_own = lax.dynamic_slice_in_dim(seq_tokens, q_start, share, 0)
    a_own = lax.dynamic_slice_in_dim(a_in, q_start, share, 0)
    seg_q = lax.dynamic_slice_in_dim(seq_seg, q_start, share, 0)[:, None]
    seg_k = seq_seg[None, :]

    padded = jnp.pad(rel_bucket, (0, 1), constant_values=bucket_count)
    roll_start = lax.rem(3 * length - 1 - share - q_start, 2 * length)
    rolled = lax.dynamic_slice_in_dim(
        jnp.concatenate([padded, padded]), roll_start, 2 * length, 0
    )
    bucket_hot = (rolled[None, :] == jnp.arange(bucket_count, dtype=jnp.int32)[:, None]).astype(
        jnp.float32
    )
    bias_rows = jnp.dot(table_all, bucket_hot, precision=HIGHEST_PRECISE)[:, None, :]

    def project(rows, weight):
        return jnp.einsum(
            "td,fd->tf", rows, weight, preferred_element_type=jnp.float32
        ).astype(jnp.bfloat16)

    queries = project(a_own, qkv_all[0])
    keys = project(a_in, qkv_all[1])
    values = project(a_in, qkv_all[2])
    mixed, lse = attend_forward(queries, keys, values, bias_rows, seg_q, seg_k, hs)
    attn = jnp.einsum("tf,fd->td", mixed, w_out_all, preferred_element_type=jnp.float32)
    residual = x_own + attn
    moe_in = normed(residual, gain_two).astype(jnp.bfloat16)
    router_f = w_router.astype(jnp.float32)
    route_own = own(routes.reshape(tok_count))
    chosen = (route_own[:, None] == jnp.arange(experts, dtype=jnp.int32)[None, :]).astype(
        jnp.float32
    )

    def gate_of(rows_in, router_in):
        logits = jnp.dot(rows_in, router_in, precision=HIGHEST_PRECISE)
        return jnp.sum(jax.nn.softmax(logits, axis=-1) * chosen, axis=-1)

    gate_value, gate_back = jax.vjp(gate_of, moe_in.astype(jnp.float32), router_f)
    grad_output = own(cotangent.reshape(tok_count, model_width)).astype(jnp.float32)
    d_rows_tok = (gate_value[:, None] * grad_output).astype(jnp.bfloat16)

    direct = slots == share and peers == 2 and experts == 2
    here = lax.axis_index("expert")
    swap = [(0, 1), (1, 0)]
    if direct:
        at_self = (route_own == here)[:, None]

        def to_slots(rows_tok):
            none = jnp.zeros_like(rows_tok)
            return (jnp.where(at_self, rows_tok, none), jnp.where(at_self, none, rows_tok))

        def from_slots(rows_slot):
            return jnp.where(at_self, rows_slot[0], rows_slot[1]).astype(jnp.float32)

    elif slots == share:
        chosen_b = chosen.astype(jnp.bfloat16)

        def to_slots(rows_tok):
            return jnp.stack([rows_tok * chosen_b[:, e : e + 1] for e in range(experts)])

        def from_slots(rows_slot):
            total = rows_slot[0].astype(jnp.float32) * chosen[:, 0:1]
            for e in range(1, experts):
                total = total + rows_slot[e].astype(jnp.float32) * chosen[:, e : e + 1]
            return total

    else:
        tok_pos = jnp.arange(share, dtype=jnp.int32)
        earlier = (tok_pos[:, None] > tok_pos[None, :]).astype(jnp.bfloat16)
        before = jnp.dot(earlier, chosen.astype(jnp.bfloat16), preferred_element_type=jnp.float32)
        slot_rank = jnp.sum(before * chosen, axis=1).astype(jnp.int32)
        place = route_own * slots + slot_rank
        place_hot = (
            place[:, None] == jnp.arange(experts * slots, dtype=jnp.int32)[None, :]
        ).astype(jnp.bfloat16)

        def to_slots(rows_tok):
            return (
                jnp.einsum("tp,td->pd", place_hot, rows_tok, preferred_element_type=jnp.float32)
                .astype(jnp.bfloat16)
                .reshape(experts, slots, model_width)
            )

        def from_slots(rows_slot):
            return jnp.einsum(
                "tp,pd->td",
                place_hot,
                rows_slot.reshape(experts * slots, model_width),
                preferred_element_type=jnp.float32,
            )

    def exchange(rows):
        if direct:
            return jnp.stack([rows[0], lax.ppermute(rows[1], "expert", swap)])
        return lax.all_to_all(rows, "expert", split_axis=0, concat_axis=0, tiled=True)

    sent_rows = exchange(to_slots(moe_in))
    sent_grad = exchange(to_slots(d_rows_tok))
    slot_total = peers * slots
    w_in_e = w_in_all.reshape(splits * ff_here, local_exp, model_width)
    w_eout_e = w_eout_all.reshape(splits * ff_here, local_exp, model_width)
    expert_in = sent_rows.reshape(peers, local_exp, slots, model_width)
    grad_rows = sent_grad.reshape(peers, local_exp, slots, model_width)

    def narrow_dot(left, right):
        return jnp.einsum("cf,fd->cd", left, right, preferred_element_type=jnp.float32).astype(
            jnp.bfloat16
        )

    def back_rows(left, right):
        if direct:
            away = lax.ppermute(narrow_dot(left[slots:], right), "expert", swap)
            return (narrow_dot(left[:slots], right), away)
        return narrow_dot(left, right).reshape(peers, 1, slots, model_width)

    out_list, row_list, gin_list, gout_list = [], [], [], []
    for e in range(local_exp):
        wi = w_in_e[:, e]
        wo = w_eout_e[:, e]
        rows_e = expert_in[:, e].reshape(slot_total, model_width)
        grad_e = grad_rows[:, e].reshape(slot_total, model_width)
        hidden = jnp.einsum("cd,fd->cf", rows_e, wi, preferred_element_type=jnp.float32)
        active = smooth(hidden).astype(jnp.bfloat16)
        out_list.append(back_rows(active, wo))
        d_active = jnp.einsum("cd,fd->cf", grad_e, wo, preferred_element_type=jnp.float32)
        d_hidden = jax.vjp(smooth, hidden)[1](d_active)[0].astype(jnp.bfloat16)
        row_list.append(back_rows(d_hidden, wi))
        gout_list.append(
            jnp.einsum("cd,cf->df", grad_e, active, preferred_element_type=jnp.float32).astype(
                jnp.bfloat16
            )
        )
        gin_list.append(
            jnp.einsum("cd,cf->df", rows_e, d_hidden, preferred_element_type=jnp.float32).astype(
                jnp.bfloat16
            )
        )

    def home(parts):
        if direct:
            return parts[0]
        return exchange(jnp.concatenate(parts, 1).reshape(experts, slots, model_width))

    returned = home(out_list)
    row_back = home(row_list)
    expert_rows = from_slots(returned)
    output_own = (residual + gate_value[:, None] * expert_rows).astype(jnp.bfloat16)
    output = lax.all_gather(output_own, "tensor", axis=0, tiled=True).reshape(tokens.shape)
    d_gate = jnp.sum(grad_output * expert_rows, axis=-1)
    d_router_in, d_router = gate_back(d_gate)
    d_moe = from_slots(row_back) + d_router_in
    d_resid_norm, d_gain_two = jax.vjp(normed, residual, gain_two)[1](d_moe)
    d_residual = grad_output + d_resid_norm
    d_attn_out = d_residual.astype(jnp.bfloat16)
    d_mixed = jnp.einsum(
        "td,fd->tf", d_attn_out, w_out_all, preferred_element_type=jnp.float32
    ).astype(jnp.bfloat16)

    grad_w_out = jnp.einsum("td,tf->df", d_attn_out, mixed, preferred_element_type=jnp.float32)
    groups = ("dp", "expert")
    group_count = lax.axis_size("dp") * peers
    part = model_width // group_count

    def by_shard(grad, columns):
        sent = grad.astype(jnp.bfloat16).reshape(group_count, part, columns, splits, head_feat)
        sent = jnp.transpose(sent, (0, 3, 1, 2, 4))
        return sent.reshape(group_count, splits, part, columns * head_feat)

    def dense_total(sent):
        sent = sent.reshape(group_count * splits * part, -1)
        over = lax.psum_scatter(sent, groups, scatter_dimension=0, tiled=True)
        over = lax.psum_scatter(over, "tensor", scatter_dimension=0, tiled=True)
        return over.astype(jnp.float32)

    def over_dp(grads):
        per = grads[0][None] if local_exp == 1 else jnp.stack(grads, 0)
        return lax.psum_scatter(per, "dp", scatter_dimension=1, tiled=True)

    def over_tensor(summed):
        summed = summed.reshape(local_exp, summed.shape[1], splits, ff_here)
        summed = jnp.transpose(summed, (2, 0, 1, 3))
        summed = lax.psum_scatter(summed, "tensor", scatter_dimension=0, tiled=True)
        return summed[0].astype(jnp.float32)

    out_sent = by_shard(grad_w_out, 1)
    d_mixed, out_sent, gout_list, gin_list, output = lax.optimization_barrier(
        (d_mixed, out_sent, gout_list, gin_list, output)
    )
    gout_dp = over_dp(gout_list)
    gin_dp = over_dp(gin_list)
    out_total = dense_total(out_sent)

    d_queries, dk_t, dv_t, d_rel = attend_backward(
        queries, keys, values, d_mixed, bias_rows, seg_q, seg_k, lse, hs
    )
    dk_t, dv_t, d_queries, gout_dp = lax.optimization_barrier((dk_t, dv_t, d_queries, gout_dp))

    def key_part(index):
        at = index * share
        return (
            lax.dynamic_slice_in_dim(dk_t, at, share, 1),
            lax.dynamic_slice_in_dim(dv_t, at, share, 1),
        )

    mine = key_part(seq_rank)
    for step in range(1, per_seq):
        sends = [
            (r, r // per_seq * per_seq + (r % per_seq + step) % per_seq) for r in range(splits)
        ]
        piece = key_part((seq_rank + step) % per_seq)
        piece = jnp.concatenate([half.astype(jnp.bfloat16) for half in piece], 0)
        piece = lax.ppermute(piece, "tensor", sends).astype(jnp.float32)
        mine = (mine[0] + piece[:feats], mine[1] + piece[feats:])
    dkv_own = [half.astype(jnp.bfloat16) for half in mine]
    dkv_own, gin_dp = lax.optimization_barrier((dkv_own, gin_dp))
    grad_eout_total = over_tensor(gout_dp)
    grad_in_total = over_tensor(gin_dp)
    grad_q = jnp.einsum("td,tf->df", a_own, d_queries, preferred_element_type=jnp.float32)
    grad_k = jnp.einsum("td,ft->df", a_own, dkv_own[0], preferred_element_type=jnp.float32)
    grad_v = jnp.einsum("td,ft->df", a_own, dkv_own[1], preferred_element_type=jnp.float32)
    d_in_total = (
        jnp.einsum("tf,fd->td", d_queries, qkv_all[0], preferred_element_type=jnp.float32)
        + jnp.einsum("ft,fd->td", dkv_own[0], qkv_all[1], preferred_element_type=jnp.float32)
        + jnp.einsum("ft,fd->td", dkv_own[1], qkv_all[2], preferred_element_type=jnp.float32)
    )
    d_inputs, d_gain_one = jax.vjp(normed, x_own, gain_one)[1](d_in_total)
    grad_own = (d_inputs + d_residual).astype(jnp.bfloat16)
    input_grad = lax.all_gather(grad_own, "tensor", axis=0, tiled=True).reshape(tokens.shape)

    width = 2 * length
    unskewed = d_rel[:, 0]
    for a in range(1, 8):
        unskewed = unskewed + jnp.pad(d_rel[:, a, a:], ((0, 0), (0, a)))
    grad_table_all = lax.dot_general(
        bucket_hot, unskewed, (((1,), (1,)), ((), ())), precision=HIGHEST_PRECISE
    )

    table_cols = -(-bucket_count * heads_here // part)
    table_sent = jnp.transpose(grad_table_all.reshape(bucket_count, splits, heads_here), (1, 0, 2))
    table_sent = table_sent.reshape(splits, bucket_count * heads_here)
    table_sent = jnp.pad(table_sent, ((0, 0), (0, table_cols * part - bucket_count * heads_here)))
    table_sent = table_sent.reshape(1, splits, part, table_cols)
    gain_sent = jnp.concatenate([d_gain_one[:, None], d_gain_two[:, None], d_router], 1)
    gain_cols = 2 + experts
    gain_sent = gain_sent.reshape(group_count, 1, part, gain_cols)
    sent = jnp.concatenate(
        [by_shard(grad, 1) for grad in (grad_q, grad_k, grad_v)]
        + [
            jnp.broadcast_to(gain_sent, (group_count, splits, part, gain_cols)).astype(
                jnp.bfloat16
            ),
            jnp.broadcast_to(table_sent, (group_count, splits, part, table_cols)).astype(
                jnp.bfloat16
            ),
        ],
        -1,
    )
    sums = dense_total(sent)
    qkv_cols = 3 * head_feat
    qkv_total = sums[:, :qkv_cols].reshape(part, 3, head_feat)
    gains = sums[:, qkv_cols : qkv_cols + gain_cols]
    table_total = sums[:, qkv_cols + gain_cols :].reshape(-1)[: bucket_count * heads_here]
    return (
        output,
        input_grad,
        gains[:, 0],
        qkv_total,
        out_total,
        table_total.reshape(bucket_count, heads_here),
        gains[:, 1],
        gains[:, 2:],
        grad_in_total,
        grad_eout_total,
    )


def solution(mesh):
    placed = (
        P(("dp", "expert"), None, None),
        P(("dp", "expert"), None),
        P(("dp", "expert"), None, None),
        P(),
        P(),
        P(None, None, "tensor"),
        P(None, "tensor"),
        P(None, "tensor"),
        P(),
        P(),
        P("expert", None, "tensor"),
        P("expert", None, "tensor"),
        P(("dp", "expert"), None, None),
    )
    return jax.shard_map(
        per_device,
        mesh=mesh,
        in_specs=placed,
        out_specs=(
            P(("dp", "expert"), None, None),
            P(("dp", "expert"), None, None),
            P(("dp", "expert")),
            P(("dp", "expert"), None, "tensor"),
            P(("dp", "expert"), "tensor"),
            P(None, "tensor"),
            P(("dp", "expert")),
            P(("dp", "expert"), None),
            P("expert", "dp", "tensor"),
            P("expert", "dp", "tensor"),
        ),
        check_vma=False,
    )
```
